512 devices in a mesh: blk: 8 (over y, core), sp: 64 (over z, x).
Axes of the slice: x: 4, y: 4, z: 16, core: 2. Of those that a mesh axis runs over, the one named last changes fastest.
Arguments:
- snapshots: float32 [64, 256, 32768], P('blk', None, 'sp'), may hold values from -6 to 6
- weights: float32 [32768], P('sp'), may hold values from 0.25 to 4
- counts: int32 [128], P('blk'), may hold values from 1 to 16
Outputs:
- modes: bfloat16 [128, 2, 16, 32768], P('blk', None, None, 'sp')
- values: float32 [128, 16], P('blk')
The draws below stay inside these ranges and needn't reach their ends.
All inputs are finite; a program needn't handle non-finite values.
Results may differ from the reference program's by a relative error of at most 0.01.
Values may be sent and summed in bfloat16 or wider, within the bound.
No kernel may reach another device: no remote copies, remote signals or barrier semaphores. Data moves between devices by JAX's collectives and lax.ppermute only.
A program may use at most 64 MiB of HBM per device.

```python
import math
import jax
import jax.numpy as jnp
from jax import lax

NT = 256
KM = 16
ITERS = 3
NB = 64
NF = 128
POINTS = 32768


def touch_ends(values, stream_key, low, largest):
    index_at = [jax.random.randint(jax.random.fold_in(stream_key, axis), (), 0, length) for axis, length in enumerate(values.shape)]
    longest = values.shape.index(max(values.shape))
    beside = index_at[:longest] + [(index_at[longest] + 1) % values.shape[longest]] + index_at[longest + 1:]
    return values.at[tuple(index_at)].set(low).at[tuple(beside)].set(largest)


def shard_levels(rng, dims, shards, least, largest):
    factor_of, own = 1.0, jax.random.fold_in(rng, 6)
    for position, shards_of in shards:
        heights = jnp.exp(jax.random.uniform(jax.random.fold_in(own, position), (shards_of,), jnp.float32, least / len(shards), largest / len(shards)))
        factor_of = factor_of * jnp.repeat(heights, dims[position] // shards_of).reshape([-1 if axis == position else 1 for axis in range(len(dims))])
    return factor_of


def gaussian(own_key, extent, scale, bound, cuts=(), held_as=jnp.bfloat16):
    level = shard_levels(own_key, extent, cuts, -0.22, 0.18) if cuts else 1.0
    entries = jax.random.normal(own_key, extent, jnp.float32) * scale * level
    return jnp.minimum(jnp.maximum(entries, -bound), bound).astype(held_as)


def setup_inputs(seed: int = 0) -> dict:
    splits = jax.random.split(jax.random.key(seed), 4)
    return {
        "snapshots": gaussian(splits[0], (NB, NT, POINTS), 1.0, 6.0, ((0, 8), (2, 64)), jnp.float32),
        "weights": jnp.clip(jnp.exp(math.log(4.0) - 2.7725887 * jax.random.uniform(splits[1], (POINTS,), jnp.float32) ** shard_levels(splits[1], (POINTS,), ((0, 64),), -0.2, 0.2)), 0.25, 4.0),
        "counts": touch_ends(jax.random.randint(splits[2], (NF,), 1, KM + 1), jax.random.fold_in(splits[2], 1), 1, KM).astype(jnp.int32),
    }


def make_table(freqs, steps):
    times = jnp.arange(steps, dtype=jnp.int32)
    rows = jnp.arange(freqs, dtype=jnp.int32)
    phase = (rows[:, None] * times[None, :] % steps).astype(jnp.float32)
    angle = 2.0 * jnp.pi * phase / steps
    window = jnp.sqrt(8.0 / (3.0 * steps)) * 0.5 * (1.0 - jnp.cos(2.0 * jnp.pi * times.astype(jnp.float32) / steps))
    return jnp.stack([jnp.cos(angle) * window, -jnp.sin(angle) * window], 1)

def reference(snapshots, weights, counts):
    table = make_table(NF, NT)
    high = lax.Precision.HIGHEST

    def one_freq(items):
        rows, count = items
        spec = jnp.einsum('ct,btp->bcp', rows, snapshots, precision=high).astype(jnp.bfloat16)
        weighted = (spec.astype(jnp.float32) * weights).astype(jnp.bfloat16)
        spec_f = spec.astype(jnp.float32)
        weighted_f = weighted.astype(jnp.float32)
        flipped = jnp.stack([spec_f[:, 1], -spec_f[:, 0]], 1)
        gram_real = jnp.einsum('bcp,dcp->bd', weighted_f, spec_f, precision=high) / POINTS
        gram_imag = jnp.einsum('bcp,dcp->bd', weighted_f, flipped, precision=high) / POINTS
        upper = jnp.concatenate([gram_real, -gram_imag], 1)
        lower_rows = jnp.concatenate([gram_imag, gram_real], 1)
        embedded = jnp.concatenate([upper, lower_rows], 0)
        basis = embedded[:, :KM]
        for step in range(ITERS):
            image = jnp.dot(embedded, basis, precision=high)
            cross = jnp.dot(image.T, image, precision=high)
            factor = jnp.linalg.cholesky(cross)
            basis = jax.scipy.linalg.solve_triangular(factor, image.T, lower=True).T
        quotient = lax.optimization_barrier(jnp.sum(basis * jnp.dot(embedded, basis, precision=high), 0))
        coef = basis.astype(jnp.bfloat16).astype(jnp.float32)
        coef_re = coef[:NB]
        coef_im = coef[NB:]
        field_re = jnp.einsum('bp,bj->jp', spec_f[:, 0], coef_re, precision=high) - jnp.einsum('bp,bj->jp', spec_f[:, 1], coef_im, precision=high)
        field_im = jnp.einsum('bp,bj->jp', spec_f[:, 1], coef_re, precision=high) + jnp.einsum('bp,bj->jp', spec_f[:, 0], coef_im, precision=high)
        energy = lax.optimization_barrier(jnp.sum(weights * (field_re * field_re + field_im * field_im), 1)) / POINTS
        keep = jnp.arange(KM, dtype=jnp.int32) < count
        scale = jnp.where(keep, 1.0 / jnp.sqrt(energy + 1e-06), 0.0)
        modes = (jnp.stack([field_re, field_im], 0) * scale[None, :, None]).astype(jnp.bfloat16)
        return (modes, jnp.where(keep, quotient, 0.0))
    return lax.map(one_freq, (table, counts))
```

```python
import functools

import jax
import jax.numpy as jnp
import ml_dtypes
import numpy as np
from jax import lax
from jax.experimental import pallas as pl
from jax.experimental.pallas import tpu as pltpu
from jax.sharding import PartitionSpec as P

KM = 16
F32 = jnp.float32
BF16 = jnp.bfloat16
NN = (((1,), (0,)), ((), ()))
NT = (((1,), (1,)), ((), ()))
VMEM_LIMIT = 48 * 1024 * 1024


def make_table(freqs, steps):
    times = np.arange(steps)
    phase = (np.arange(freqs)[:, None] * times[None, :]) % steps
    angle = 2.0 * np.pi * phase / steps
    window = np.sqrt(8.0 / (3.0 * steps)) * 0.5 * (1.0 - np.cos(2.0 * np.pi * times / steps))
    table = np.stack([np.cos(angle) * window, np.sin(angle) * window], 1)
    table = table.reshape(2 * freqs, steps).astype(np.float32)
    high = table.astype(ml_dtypes.bfloat16)
    low = (table - high.astype(np.float32)).astype(ml_dtypes.bfloat16)
    return high, low


def split(x):
    high = x.astype(BF16)
    return high, (x - high.astype(F32)).astype(BF16)


def mm(a, b, dims=NN, precision=None):
    return lax.dot_general(a, b, dims, preferred_element_type=F32, precision=precision)


def dft_kernel(high_ref, low_ref, x_ref, out_ref, acc_ref):
    blocks = x_ref.shape[0]
    rows = high_ref.shape[0]
    high, low = high_ref[...], low_ref[...]
    for b in range(blocks):
        xh, xl = split(x_ref[b])
        acc = mm(high, xh) + mm(high, xl) + mm(low, xh)
        for col in range(0, acc.shape[1], 128):
            acc_ref[col // 128, pl.ds(b, rows, stride=blocks), :] = acc[:, col : col + 128]
    for col in range(0, out_ref.shape[1], 128):
        out_ref[:, col : col + 128] = acc_ref[col // 128].astype(BF16)


def dft(snapshots, freqs):
    blocks, steps, pts = snapshots.shape
    high, low = make_table(freqs, steps)
    wide = 256
    rows = 2 * freqs
    return pl.pallas_call(
        dft_kernel,
        grid=(pts // wide,),
        in_specs=[
            pl.BlockSpec((rows, steps), lambda i: (0, 0)),
            pl.BlockSpec((rows, steps), lambda i: (0, 0)),
            pl.BlockSpec((blocks, steps, wide), lambda i: (0, 0, i)),
        ],
        out_specs=pl.BlockSpec((rows * blocks, wide), lambda i: (0, i)),
        out_shape=jax.ShapeDtypeStruct((rows * blocks, pts), BF16),
        scratch_shapes=[pltpu.VMEM((wide // 128, rows * blocks, 128), F32)],
        compiler_params=pltpu.CompilerParams(vmem_limit_bytes=VMEM_LIMIT),
        name="dft",
    )(jnp.asarray(high), jnp.asarray(low), snapshots)


def exchange(x, sign_first):
    lane = lax.broadcasted_iota(jnp.int32, x.shape, x.ndim - 1)
    last = x.ndim - 1
    up = pltpu.roll(x, 120, last)
    down = pltpu.roll(x, 8, last)
    if sign_first:
        return jnp.where((lane & 8) == 0, -up, down)
    return jnp.where((lane & 8) == 0, up, -down)


def gram_kernel(points_all, z_ref, w_ref, out_ref):
    groups, freqs, pairs, pts = z_ref.shape
    weights = w_ref[...]
    for f in range(freqs):
        z = z_ref[:, f].reshape(groups * pairs, pts)
        zw = (z.astype(F32) * weights).astype(BF16)
        m = mm(zw, z, NT).reshape(groups, 2, pairs // 2, 128)
        top = m[:, 0].reshape(groups * pairs // 2, 128)
        bottom = m[:, 1].reshape(groups * pairs // 2, 128)
        out_ref[f] = (top + exchange(bottom, False)) * (1.0 / points_all)


def gram(own, weights, points_all):
    groups, freqs, pairs, pts = own.shape
    return pl.pallas_call(
        functools.partial(gram_kernel, points_all),
        in_specs=[pl.BlockSpec(memory_space=pltpu.VMEM)] * 2,
        out_specs=pl.BlockSpec(memory_space=pltpu.VMEM),
        out_shape=jax.ShapeDtypeStruct((freqs, groups * pairs // 2, 128), F32),
        compiler_params=pltpu.CompilerParams(vmem_limit_bytes=VMEM_LIMIT),
        name="gram",
    )(own, weights.reshape(1, pts))


def inverse_factor(cross):
    row = lax.broadcasted_iota(jnp.int32, cross.shape, 0)
    lane = lax.broadcasted_iota(jnp.int32, cross.shape, 1)
    inv = jnp.where((lane & (KM - 1)) == row, 1.0, 0.0)
    pivots = jnp.ones_like(cross)
    for k in range(KM):
        column = jnp.take_along_axis(cross, (lane & ~(KM - 1)) + k, axis=1)
        pivot = jnp.broadcast_to(column[k : k + 1], cross.shape)
        pivots = jnp.where(row == k, pivot, pivots)
        if k < KM - 1:
            factor = jnp.where(row > k, column / pivot, 0.0)
            cross = cross - factor * cross[k : k + 1]
            inv = inv - factor * inv[k : k + 1]
    return inv * lax.rsqrt(pivots)


def orthonormal(image):
    high = lax.Precision.HIGHEST
    product = mm(image, image, NT, high)
    lane = lax.broadcasted_iota(jnp.int32, (KM, 128), 1)
    cross = jnp.zeros((KM, 128), F32)
    for f in range(128 // KM):
        cross = jnp.where(lane // KM == f, product[f * KM : (f + 1) * KM], cross)
    inv = inverse_factor(cross)
    wide = jnp.concatenate([inv] * (128 // KM), 0)
    row = lax.broadcasted_iota(jnp.int32, wide.shape, 0)
    column = lax.broadcasted_iota(jnp.int32, wide.shape, 1)
    wide = jnp.where(row // KM == column // KM, wide, 0.0)
    return mm(wide, image, NN, high)


def modes_kernel(counts_ref, g_ref, z_hbm, modes_ref, values_ref, z_ref, e_ref, sem):
    groups, freqs, pairs, pts = z_hbm.shape
    fetch = pltpu.make_async_copy(z_hbm, z_ref, sem)
    fetch.start()
    for f in range(freqs):
        top = g_ref[f]
        bottom = exchange(top, True)
        shape = (groups, pairs // 2, 128)
        e = jnp.stack([top.reshape(shape), bottom.reshape(shape)], 1).reshape(128, 128)
        eh, el = split(e)
        e_ref[f, :, :128] = eh
        e_ref[f, :, 128:] = el

    def times_e(basis, f):
        high, low = split(basis)
        r = mm(jnp.concatenate([high, low], 0), e_ref[f])
        return r[:KM, :128] + (r[KM:, :128] + r[:KM, 128:])

    def rows(x, f):
        half = 128 // KM
        return x[f // half][(f % half) * KM : (f % half + 1) * KM]

    def halves(pieces):
        half = 128 // KM
        return [jnp.concatenate(pieces[i : i + half], 0) for i in range(0, freqs, half)]

    image = halves([times_e(g_ref[f, :KM], f) for f in range(freqs)])
    basis = [orthonormal(x) for x in image]
    image = halves([times_e(times_e(rows(basis, f), f), f) for f in range(freqs)])
    basis = [orthonormal(x) for x in image]

    row = lax.broadcasted_iota(jnp.int32, (KM, 128), 0)
    lane = lax.broadcasted_iota(jnp.int32, (KM, 128), 1)
    quotients = jnp.zeros((KM, 128), F32)
    fetch.wait()
    for f in range(freqs):
        b = rows(basis, f)
        high, low = split(b)
        coef = high.astype(F32)
        r = mm(jnp.concatenate([high, low], 0), e_ref[f])
        e_coef = r[:KM, :128] + r[:KM, 128:]
        e_basis = e_coef + r[KM:, :128]
        keep = row[:, :1] < counts_ref[f]
        quotient = jnp.sum(b * e_basis, 1, keepdims=True)
        energy = jnp.sum(coef * e_coef, 1, keepdims=True)
        quotients = jnp.where(lane == f, jnp.where(keep, quotient, 0.0), quotients)
        scale = jnp.where(keep, lax.rsqrt(energy + 1e-06), 0.0)
        both = jnp.concatenate([coef, exchange(coef, False)], 0).astype(BF16)
        field = mm(both, z_ref[:, f].reshape(groups * pairs, pts))
        modes_ref[f] = (field * jnp.concatenate([scale, scale], 0)).astype(BF16)
    padded = jnp.concatenate([quotients] * (128 // KM), 0)
    values_ref[...] = padded.T[:freqs, :KM]


def modes_and_values(counts, g, own):
    groups, freqs, pairs, pts = own.shape
    vmem = pl.BlockSpec(memory_space=pltpu.VMEM)
    return pl.pallas_call(
        modes_kernel,
        in_specs=[
            pl.BlockSpec(memory_space=pltpu.SMEM),
            vmem,
            pl.BlockSpec(memory_space=pl.ANY),
        ],
        out_specs=[vmem, vmem],
        out_shape=[
            jax.ShapeDtypeStruct((freqs, 2 * KM, pts), BF16),
            jax.ShapeDtypeStruct((freqs, KM), F32),
        ],
        scratch_shapes=[
            pltpu.VMEM(own.shape, BF16),
            pltpu.VMEM((freqs, 128, 256), BF16),
            pltpu.SemaphoreType.DMA,
        ],
        compiler_params=pltpu.CompilerParams(vmem_limit_bytes=VMEM_LIMIT),
        name="modes",
    )(counts, g, own)


def local(snapshots, weights, counts):
    blk_dev, steps, pts = snapshots.shape
    groups = lax.axis_size("blk")
    band = counts.shape[0]
    freqs = band * groups
    points_all = pts * lax.axis_size("sp")
    spectra = dft(snapshots, freqs).reshape(groups, band, 2 * blk_dev, pts)
    own = lax.all_to_all(spectra, "blk", split_axis=0, concat_axis=0, tiled=True)
    total = lax.psum(gram(own, weights, points_all), "sp")
    modes, values = modes_and_values(counts, total, own)
    return modes.reshape(band, 2, KM, pts), values


def solution(mesh):
    in_specs = (P("blk", None, "sp"), P("sp"), P("blk"))
    out_specs = (P("blk", None, None, "sp"), P("blk", None))
    return jax.shard_map(local, mesh=mesh, in_specs=in_specs, out_specs=out_specs, check_vma=False)
```

```python
import functools

import jax
import jax.numpy as jnp
import ml_dtypes
import numpy as np
from jax import lax
from jax.experimental import pallas as pl
from jax.experimental.pallas import tpu as pltpu
from jax.sharding import PartitionSpec as P

KM = 16
F32 = jnp.float32
BF16 = jnp.bfloat16
NN = (((1,), (0,)), ((), ()))
NT = (((1,), (1,)), ((), ()))
VMEM_LIMIT = 48 * 1024 * 1024


def make_table(freqs, steps):
    times = np.arange(steps)
    phase = (np.arange(freqs)[:, None] * times[None, :]) % steps
    angle = 2.0 * np.pi * phase / steps
    window = np.sqrt(8.0 / (3.0 * steps)) * 0.5 * (1.0 - np.cos(2.0 * np.pi * times / steps))
    table = np.stack([np.cos(angle) * window, np.sin(angle) * window], 1)
    table = table.reshape(2 * freqs, steps).astype(np.float32)
    high = table.astype(ml_dtypes.bfloat16)
    low = (table - high.astype(np.float32)).astype(ml_dtypes.bfloat16)
    return high, low


def split(x):
    high = x.astype(BF16)
    return high, (x - high.astype(F32)).astype(BF16)


def mm(a, b, dims=NN, precision=None):
    return lax.dot_general(a, b, dims, preferred_element_type=F32, precision=precision)


def dft_kernel(high_ref, low_ref, x_ref, out_ref, acc_ref):
    blocks = x_ref.shape[0]
    rows = high_ref.shape[0]
    high, low = high_ref[...], low_ref[...]
    for b in range(blocks):
        xh, xl = split(x_ref[b])
        acc = mm(high, xh) + mm(high, xl) + mm(low, xh)
        for col in range(0, acc.shape[1], 128):
            acc_ref[col // 128, pl.ds(b, rows, stride=blocks), :] = acc[:, col : col + 128]
    for col in range(0, out_ref.shape[1], 128):
        out_ref[:, col : col + 128] = acc_ref[col // 128].astype(BF16)


def dft(snapshots, freqs):
    blocks, steps, pts = snapshots.shape
    high, low = make_table(freqs, steps)
    wide = 256
    rows = 2 * freqs
    return pl.pallas_call(
        dft_kernel,
        grid=(pts // wide,),
        in_specs=[
            pl.BlockSpec((rows, steps), lambda i: (0, 0)),
            pl.BlockSpec((rows, steps), lambda i: (0, 0)),
            pl.BlockSpec((blocks, steps, wide), lambda i: (0, 0, i)),
        ],
        out_specs=pl.BlockSpec((rows * blocks, wide), lambda i: (0, i)),
        out_shape=jax.ShapeDtypeStruct((rows * blocks, pts), BF16),
        scratch_shapes=[pltpu.VMEM((wide // 128, rows * blocks, 128), F32)],
        compiler_params=pltpu.CompilerParams(vmem_limit_bytes=VMEM_LIMIT),
        name="dft",
    )(jnp.asarray(high), jnp.asarray(low), snapshots)


def exchange(x, sign_first):
    lane = lax.broadcasted_iota(jnp.int32, x.shape, x.ndim - 1)
    last = x.ndim - 1
    up = pltpu.roll(x, 120, last)
    down = pltpu.roll(x, 8, last)
    if sign_first:
        return jnp.where((lane & 8) == 0, -up, down)
    return jnp.where((lane & 8) == 0, up, -down)


def places(rows):
    row = lax.broadcasted_iota(jnp.int32, (rows, 128), 0)
    lane = lax.broadcasted_iota(jnp.int32, (rows, 128), 1)
    return row, (lane >> 4) * 8 + (lane & 7), (lane & 8) == 0


def gram_kernel(points_all, z_ref, w_ref, out_ref):
    groups, freqs, pairs, pts = z_ref.shape
    weights = w_ref[...]
    rows = groups * pairs // 2
    row, block, first = places(rows)

    def one(f):
        z = z_ref[:, f].reshape(groups * pairs, pts)
        zw = (z.astype(F32) * weights).astype(BF16)
        m = mm(zw, z, NT).reshape(groups, 2, pairs // 2, 128)
        top = m[:, 0].reshape(rows, 128)
        bottom = m[:, 1].reshape(rows, 128)
        return (top + exchange(bottom, False)) * (1.0 / points_all)

    for f in range(0, freqs, 2):
        a, b = one(f), one(f + 1)
        a = jnp.where(row <= block, a, pltpu.roll(a, 120, 1))
        b = jnp.where(row <= block, pltpu.roll(b, 8, 1), b)
        out_ref[f // 2] = jnp.where(first, a, b)


def gram(own, weights, points_all):
    groups, freqs, pairs, pts = own.shape
    return pl.pallas_call(
        functools.partial(gram_kernel, points_all),
        in_specs=[pl.BlockSpec(memory_space=pltpu.VMEM)] * 2,
        out_specs=pl.BlockSpec(memory_space=pltpu.VMEM),
        out_shape=jax.ShapeDtypeStruct((freqs // 2, groups * pairs // 2, 128), F32),
        compiler_params=pltpu.CompilerParams(vmem_limit_bytes=VMEM_LIMIT),
        name="gram",
    )(own, weights.reshape(1, pts))


def total_kernel(x_ref, out_ref):
    total = jnp.sum(x_ref[...], 0)
    for i in range(out_ref.shape[0]):
        out_ref[i] = total


def total_for(x, copies):
    return pl.pallas_call(
        total_kernel,
        in_specs=[pl.BlockSpec(memory_space=pltpu.VMEM)],
        out_specs=pl.BlockSpec(memory_space=pltpu.VMEM),
        out_shape=jax.ShapeDtypeStruct((copies,) + x.shape[1:], F32),
        compiler_params=pltpu.CompilerParams(vmem_limit_bytes=VMEM_LIMIT),
        name="total",
    )(x)


def sum_points(packed):
    nz, nx = lax.axis_size("z"), lax.axis_size("x")
    pieces = packed.reshape(nz * nx, -1, 128)
    pieces = lax.all_to_all(pieces, ("z", "x"), split_axis=0, concat_axis=0, tiled=True)
    mine = total_for(pieces, nz)
    column = lax.all_to_all(mine, "z", split_axis=0, concat_axis=0, tiled=True)
    columns = jnp.broadcast_to(column[None], (nx,) + column.shape)
    return lax.all_to_all(columns, "x", split_axis=0, concat_axis=0, tiled=True)


def inverse_factor(cross):
    row = lax.broadcasted_iota(jnp.int32, cross.shape, 0)
    lane = lax.broadcasted_iota(jnp.int32, cross.shape, 1)
    inv = jnp.where((lane & (KM - 1)) == row, 1.0, 0.0)
    pivots = jnp.ones_like(cross)
    for k in range(KM):
        column = jnp.take_along_axis(cross, (lane & ~(KM - 1)) + k, axis=1)
        pivot = jnp.broadcast_to(column[k : k + 1], cross.shape)
        pivots = jnp.where(row == k, pivot, pivots)
        if k < KM - 1:
            factor = jnp.where(row > k, column / pivot, 0.0)
            cross = cross - factor * cross[k : k + 1]
            inv = inv - factor * inv[k : k + 1]
    return inv * lax.rsqrt(pivots)


def orthonormal(image):
    high = lax.Precision.HIGHEST
    product = mm(image, image, NT, high)
    lane = lax.broadcasted_iota(jnp.int32, (KM, 128), 1)
    cross = jnp.zeros((KM, 128), F32)
    for f in range(128 // KM):
        cross = jnp.where(lane // KM == f, product[f * KM : (f + 1) * KM], cross)
    inv = inverse_factor(cross)
    wide = jnp.concatenate([inv] * (128 // KM), 0)
    row = lax.broadcasted_iota(jnp.int32, wide.shape, 0)
    column = lax.broadcasted_iota(jnp.int32, wide.shape, 1)
    wide = jnp.where(row // KM == column // KM, wide, 0.0)
    return mm(wide, image, NN, high)


def modes_kernel(counts_ref, g_ref, z_hbm, modes_ref, values_ref, z_ref, e_ref, sem):
    groups, freqs, pairs, pts = z_hbm.shape
    fetch = pltpu.make_async_copy(z_hbm, z_ref, sem)
    fetch.start()
    nx, nz = g_ref.shape[:2]
    row, block, first = places(groups * pairs // 2)
    upper, lower = row <= block, row > block
    tall = (groups, pairs // 2, 128)

    def piece(pair):
        per = groups * pairs // 2 // g_ref.shape[2]
        return jnp.concatenate([g_ref[i % nx, i // nx] for i in range(pair * per, (pair + 1) * per)], 0)

    starts = []
    for f in range(0, freqs, 4):
        q = [piece(f // 2), piece(f // 2 + 1)]
        t = jnp.stack([q[0].reshape(tall), q[1].reshape(tall)], 1).reshape(128, 128).T
        t = t.reshape(groups, 2, pairs // 2, 128)
        t = [t[:, 0].reshape(-1, 128), t[:, 1].reshape(-1, 128)]
        for i in range(4):
            p, pt = q[i // 2], t[i % 2]
            p = pltpu.roll(p, 120, 1) if i % 2 else p
            pt = pltpu.roll(pt, 120, 1) if i // 2 else pt
            real = jnp.where(upper, p, pt)
            imag = jnp.where(lower, -p, jnp.where(row == block, 0.0, pt))
            top = jnp.where(first, real, pltpu.roll(-imag, 8, 1))
            bottom = jnp.where(first, imag, pltpu.roll(real, 8, 1))
            starts.append(top[:KM])
            e = jnp.stack([top.reshape(tall), bottom.reshape(tall)], 1).reshape(128, 128)
            eh, el = split(e)
            e_ref[f + i, :, :128] = eh
            e_ref[f + i, :, 128:] = el

    def times_e(basis, f):
        high, low = split(basis)
        r = mm(jnp.concatenate([high, low], 0), e_ref[f])
        return r[:KM, :128] + (r[KM:, :128] + r[:KM, 128:])

    def rows(x, f):
        half = 128 // KM
        return x[f // half][(f % half) * KM : (f % half + 1) * KM]

    def halves(pieces):
        half = 128 // KM
        return [jnp.concatenate(pieces[i : i + half], 0) for i in range(0, freqs, half)]

    image = halves([times_e(starts[f], f) for f in range(freqs)])
    basis = [orthonormal(x) for x in image]
    image = halves([times_e(times_e(rows(basis, f), f), f) for f in range(freqs)])
    basis = [orthonormal(x) for x in image]

    row = lax.broadcasted_iota(jnp.int32, (KM, 128), 0)
    lane = lax.broadcasted_iota(jnp.int32, (KM, 128), 1)
    quotients = jnp.zeros((KM, 128), F32)
    fetch.wait()
    for f in range(freqs):
        b = rows(basis, f)
        high, low = split(b)
        coef = high.astype(F32)
        r = mm(jnp.concatenate([high, low], 0), e_ref[f])
        e_coef = r[:KM, :128] + r[:KM, 128:]
        e_basis = e_coef + r[KM:, :128]
        keep = row[:, :1] < counts_ref[f]
        quotient = jnp.sum(b * e_basis, 1, keepdims=True)
        energy = jnp.sum(coef * e_coef, 1, keepdims=True)
        quotients = jnp.where(lane == f, jnp.where(keep, quotient, 0.0), quotients)
        scale = jnp.where(keep, lax.rsqrt(energy + 1e-06), 0.0)
        both = jnp.concatenate([coef, exchange(coef, False)], 0).astype(BF16)
        field = mm(both, z_ref[:, f].reshape(groups * pairs, pts))
        modes_ref[f] = (field * jnp.concatenate([scale, scale], 0)).astype(BF16)
    padded = jnp.concatenate([quotients] * (128 // KM), 0)
    values_ref[...] = padded.T[:freqs, :KM]


def modes_and_values(counts, g, own):
    groups, freqs, pairs, pts = own.shape
    vmem = pl.BlockSpec(memory_space=pltpu.VMEM)
    return pl.pallas_call(
        modes_kernel,
        in_specs=[
            pl.BlockSpec(memory_space=pltpu.SMEM),
            vmem,
            pl.BlockSpec(memory_space=pl.ANY),
        ],
        out_specs=[vmem, vmem],
        out_shape=[
            jax.ShapeDtypeStruct((freqs, 2 * KM, pts), BF16),
            jax.ShapeDtypeStruct((freqs, KM), F32),
        ],
        scratch_shapes=[
            pltpu.VMEM(own.shape, BF16),
            pltpu.VMEM((freqs, 128, 256), BF16),
            pltpu.SemaphoreType.DMA,
        ],
        compiler_params=pltpu.CompilerParams(vmem_limit_bytes=VMEM_LIMIT),
        name="modes",
    )(counts, g, own)


def local(snapshots, weights, counts):
    blk_dev, steps, pts = snapshots.shape
    groups = lax.axis_size("blk")
    band = counts.shape[0]
    freqs = band * groups
    points_all = pts * lax.axis_size("z") * lax.axis_size("x")
    spectra = dft(snapshots, freqs).reshape(groups, band, 2 * blk_dev, pts)
    own = lax.all_to_all(spectra, "blk", split_axis=0, concat_axis=0, tiled=True)
    total = sum_points(gram(own, weights, points_all))
    modes, values = modes_and_values(counts, total, own)
    return modes.reshape(band, 2, KM, pts), values


def solution(mesh):
    blk, sp = mesh.devices.shape
    nx = min(4, sp)
    mesh = jax.sharding.Mesh(mesh.devices.reshape(blk, sp // nx, nx), ("blk", "z", "x"))
    points = ("z", "x")
    in_specs = (P("blk", None, points), P(points), P("blk"))
    out_specs = (P("blk", None, None, points), P("blk", None))
    return jax.shard_map(local, mesh=mesh, in_specs=in_specs, out_specs=out_specs, check_vma=False)
```

```python
import functools

import jax
import jax.numpy as jnp
import ml_dtypes
import numpy as np
from jax import lax
from jax.experimental import pallas as pl
from jax.experimental.pallas import tpu as pltpu
from jax.sharding import PartitionSpec as P

KM = 16
F32 = jnp.float32
BF16 = jnp.bfloat16
NN = (((1,), (0,)), ((), ()))
NT = (((1,), (1,)), ((), ()))
VMEM_LIMIT = 48 * 1024 * 1024


def make_table(freqs, steps):
    times = np.arange(steps)
    phase = (np.arange(freqs)[:, None] * times[None, :]) % steps
    angle = 2.0 * np.pi * phase / steps
    window = np.sqrt(8.0 / (3.0 * steps)) * 0.5 * (1.0 - np.cos(2.0 * np.pi * times / steps))
    table = np.stack([np.cos(angle) * window, np.sin(angle) * window], 1)
    table = table.reshape(2 * freqs, steps).astype(np.float32)
    high = table.astype(ml_dtypes.bfloat16)
    low = (table - high.astype(np.float32)).astype(ml_dtypes.bfloat16)
    return np.concatenate([high, low], 0)


def split(x):
    high = x.astype(BF16)
    return high, (x - high.astype(F32)).astype(BF16)


def mm(a, b, dims=NN, precision=None):
    return lax.dot_general(a, b, dims, preferred_element_type=F32, precision=precision)


def dft_kernel(table_ref, x_ref, out_ref, acc_ref):
    blocks = x_ref.shape[0]
    rows = table_ref.shape[0] // 2
    table = table_ref[...]
    high = table[:rows]
    for b in range(blocks):
        xh, xl = split(x_ref[b])
        both = mm(table, xh)
        acc = both[:rows] + (both[rows:] + mm(high, xl))
        for col in range(0, acc.shape[1], 128):
            acc_ref[col // 128, pl.ds(b, rows, stride=blocks), :] = acc[:, col : col + 128]
    for col in range(0, out_ref.shape[1], 128):
        out_ref[:, col : col + 128] = acc_ref[col // 128].astype(BF16)


def dft(snapshots, freqs):
    blocks, steps, pts = snapshots.shape
    table = make_table(freqs, steps)
    wide = 256
    rows = 2 * freqs
    return pl.pallas_call(
        dft_kernel,
        grid=(pts // wide,),
        in_specs=[
            pl.BlockSpec((2 * rows, steps), lambda i: (0, 0)),
            pl.BlockSpec((blocks, steps, wide), lambda i: (0, 0, i)),
        ],
        out_specs=pl.BlockSpec((rows * blocks, wide), lambda i: (0, i)),
        out_shape=jax.ShapeDtypeStruct((rows * blocks, pts), BF16),
        scratch_shapes=[pltpu.VMEM((wide // 128, rows * blocks, 128), F32)],
        compiler_params=pltpu.CompilerParams(vmem_limit_bytes=VMEM_LIMIT),
        name="dft",
    )(jnp.asarray(table), snapshots)


def exchange(x, sign_first):
    lane = lax.broadcasted_iota(jnp.int32, x.shape, x.ndim - 1)
    last = x.ndim - 1
    up = pltpu.roll(x, 120, last)
    down = pltpu.roll(x, 8, last)
    if sign_first:
        return jnp.where((lane & 8) == 0, -up, down)
    return jnp.where((lane & 8) == 0, up, -down)


def places(rows):
    row = lax.broadcasted_iota(jnp.int32, (rows, 128), 0)
    lane = lax.broadcasted_iota(jnp.int32, (rows, 128), 1)
    return row, (lane >> 4) * 8 + (lane & 7), (lane & 8) == 0


def gram_kernel(points_all, z_ref, w_ref, out_ref):
    groups, freqs, pairs, pts = z_ref.shape
    weights = w_ref[...]
    rows = groups * pairs // 2
    row, block, first = places(rows)
    for f in range(freqs):
        z = z_ref[:, f].reshape(groups * pairs, pts)
        zw = (z.astype(F32) * weights).astype(BF16)
        m = mm(zw, z, NT).reshape(groups, 2, pairs // 2, 128)
        top = m[:, 0].reshape(rows, 128)
        bottom = m[:, 1].reshape(rows, 128)
        g = (top + exchange(bottom, False)) * (1.0 / points_all)
        p = jnp.where(row <= block, g, pltpu.roll(g, 120, 1))
        half = rows // 2
        out_ref[f] = jnp.where(first[:half], p[:half], pltpu.roll(p[half:], 8, 1)).astype(out_ref.dtype)


def call(kernel, out_shape, *args, scratch=(), name):
    vmem = pl.BlockSpec(memory_space=pltpu.VMEM)
    smem = pl.BlockSpec(memory_space=pltpu.SMEM)
    return pl.pallas_call(
        kernel,
        in_specs=[smem if x.dtype == jnp.int32 else vmem for x in args],
        out_specs=jax.tree.map(lambda _: vmem, out_shape),
        out_shape=out_shape,
        scratch_shapes=scratch,
        compiler_params=pltpu.CompilerParams(vmem_limit_bytes=VMEM_LIMIT),
        name=name,
    )(*args)


def total_kernel(x_ref, out_ref):
    total = jnp.sum(x_ref[...].astype(F32), 0)
    for i in range(out_ref.shape[0]):
        out_ref[i] = total


def factor_out(image):
    cross = mm(image, image, NT, lax.Precision.HIGHEST)
    columns = [jnp.broadcast_to(cross[:, k : k + 1], image.shape) for k in range(KM)]
    row = lax.broadcasted_iota(jnp.int32, image.shape, 0)
    pivots = columns[KM - 1]
    for k in range(KM):
        pivot = columns[k][k : k + 1]
        pivots = jnp.where(row == k, pivot, pivots)
        if k < KM - 1:
            factor = jnp.where(row > k, columns[k] * (1.0 / pivot), 0.0)
            for j in range(k + 1, KM):
                columns[j] = columns[j] - factor * columns[j][k : k + 1]
            image = image - factor * image[k : k + 1]
    return image * lax.rsqrt(pivots)


def unpacked(s):
    half = s.shape[0]
    rows = 2 * half
    row, block, first = places(rows)
    p = jnp.concatenate([s, pltpu.roll(s, 120, 1)], 0)
    tall = (rows // 8, 8, 128)
    t = jnp.stack([p.reshape(tall), p.reshape(tall)], 1).reshape(2 * rows, 128).T
    pt = t.reshape(rows // 8, 2, 8, 128)[:, 0].reshape(rows, 128)
    real = jnp.where(row <= block, p, pt)
    imag = jnp.where(row > block, -p, jnp.where(row == block, 0.0, pt))
    top = jnp.where(first, real, pltpu.roll(-imag, 8, 1))
    bottom = jnp.where(first, imag, pltpu.roll(real, 8, 1))
    return jnp.stack([top.reshape(tall), bottom.reshape(tall)], 1).reshape(2 * rows, 128), top


def iterate_kernel(x_ref, out_ref):
    embedded, top = unpacked(jnp.sum(x_ref[...], 0))
    eh, el = split(embedded)
    e = jnp.concatenate([eh, el], 1)

    def times_e(basis):
        high, low = split(basis)
        r = mm(jnp.concatenate([high, low], 0), e)
        return r[:KM, :128], r[KM:, :128] + r[:KM, 128:]

    image = sum(times_e(top[:KM]))
    basis = factor_out(image)
    basis = factor_out(sum(times_e(sum(times_e(basis)))))
    high, low = split(basis)
    r = mm(jnp.concatenate([high, low], 0), e)
    e_coef = r[:KM, :128] + r[:KM, 128:]
    e_basis = e_coef + r[KM:, :128]
    energy = jnp.sum(high.astype(F32) * e_coef, 1, keepdims=True)
    quotient = jnp.sum(basis * e_basis, 1, keepdims=True)
    lane = lax.broadcasted_iota(jnp.int32, (KM, 128), 1)
    rest = jnp.where(lane < 3, lax.rsqrt(jnp.maximum(energy, 0.0) + 1e-06), quotient)
    first = rest.astype(BF16).astype(F32)
    second = (rest - first).astype(BF16).astype(F32)
    third = rest - first - second
    step = jnp.where(lane < 3, lane, lane - 3)
    words = jnp.where(step == 0, first, jnp.where(step == 1, second, third))
    both = jnp.concatenate([high, jnp.where(lane < 6, words, 0.0).astype(BF16)], 0)
    for i in range(out_ref.shape[0]):
        out_ref[i] = both


def modes_kernel(counts_ref, coef_ref, z_ref, modes_ref, values_ref):
    groups, freqs, pairs, pts = z_ref.shape
    row = lax.broadcasted_iota(jnp.int32, (KM, 128), 0)
    lane = lax.broadcasted_iota(jnp.int32, (KM, 128), 1)
    quotients = jnp.zeros((KM, 128), F32)
    for f in range(freqs):
        coef = coef_ref[f, :KM].astype(F32)
        words = coef_ref[f, KM:].astype(F32)
        keep = row[:, :1] < counts_ref[f]
        scale = jnp.where(keep, words[:, 0:1] + words[:, 1:2] + words[:, 2:3], 0.0)
        quotient = jnp.where(keep, words[:, 3:4] + words[:, 4:5] + words[:, 5:6], 0.0)
        quotients = jnp.where(lane == f, quotient, quotients)
        both = jnp.concatenate([coef, exchange(coef, False)], 0).astype(BF16)
        field = mm(both, z_ref[:, f].reshape(groups * pairs, pts))
        modes_ref[f] = (field * jnp.concatenate([scale, scale], 0)).astype(BF16)
    padded = jnp.concatenate([quotients] * (128 // KM), 0)
    values_ref[...] = padded.T[:freqs, :KM]


def local(snapshots, weights, counts):
    blk_dev, steps, pts = snapshots.shape
    groups = lax.axis_size("blk")
    band = counts.shape[0]
    freqs = band * groups
    nz, nx = lax.axis_size("z"), lax.axis_size("x")
    shape = jax.ShapeDtypeStruct
    spectra = dft(snapshots, freqs).reshape(groups, band, 2 * blk_dev, pts)
    own = lax.all_to_all(spectra, "blk", split_axis=0, concat_axis=0, tiled=True)
    half = groups * blk_dev // 2
    packed = call(
        functools.partial(gram_kernel, pts * nz * nx),
        shape((band, half, 128), BF16),
        own,
        weights.reshape(1, pts),
        name="gram",
    )
    parts = lax.all_to_all(packed, "z", split_axis=0, concat_axis=0, tiled=True)
    copies = call(total_kernel, shape((nx, half, 128), F32), parts, name="total")
    columns = lax.all_to_all(copies, "x", split_axis=0, concat_axis=0, tiled=True)
    mine = call(iterate_kernel, shape((nz, 2 * KM, 128), BF16), columns, name="iterate")
    coefs = lax.all_to_all(mine, "z", split_axis=0, concat_axis=0, tiled=True)
    modes, values = call(
        modes_kernel,
        [shape((band, 2 * KM, pts), BF16), shape((band, KM), F32)],
        counts,
        coefs,
        own,
        name="modes",
    )
    return modes.reshape(band, 2, KM, pts), values


def solution(mesh):
    blk, sp = mesh.devices.shape
    nx = min(4, sp)
    mesh = jax.sharding.Mesh(mesh.devices.reshape(blk, sp // nx, nx), ("blk", "z", "x"))
    points = ("z", "x")
    in_specs = (P("blk", None, points), P(points), P("blk"))
    out_specs = (P("blk", None, None, points), P("blk", None))
    return jax.shard_map(local, mesh=mesh, in_specs=in_specs, out_specs=out_specs, check_vma=False)
```

```python
import functools

import jax
import jax.numpy as jnp
import ml_dtypes
import numpy as np
from jax import lax
from jax.experimental import pallas as pl
from jax.experimental.pallas import tpu as pltpu
from jax.sharding import PartitionSpec as P

KM = 16
F32 = jnp.float32
BF16 = jnp.bfloat16
NN = (((1,), (0,)), ((), ()))
NT = (((1,), (1,)), ((), ()))
VMEM_LIMIT = 48 * 1024 * 1024


def make_table(freqs, steps):
    times = np.arange(steps)
    phase = (np.arange(freqs)[:, None] * times[None, :]) % steps
    angle = 2.0 * np.pi * phase / steps
    window = np.sqrt(8.0 / (3.0 * steps)) * 0.5 * (1.0 - np.cos(2.0 * np.pi * times / steps))
    table = np.stack([np.cos(angle) * window, np.sin(angle) * window], 1)
    table = table.reshape(2 * freqs, steps).astype(np.float32)
    high = table.astype(ml_dtypes.bfloat16)
    low = (table - high.astype(np.float32)).astype(ml_dtypes.bfloat16)
    return np.concatenate([high, low], 0)


def split(x):
    high = x.astype(BF16)
    return high, (x - high.astype(F32)).astype(BF16)


def mm(a, b, dims=NN, precision=None):
    return lax.dot_general(a, b, dims, preferred_element_type=F32, precision=precision)


def dft_kernel(table_ref, x_ref, out_ref, spectra_ref):
    blocks = x_ref.shape[0]
    rows = table_ref.shape[0] // 2
    table = table_ref[...]
    high = table[:rows]
    for b in range(blocks):
        xh, xl = split(x_ref[b])
        both = mm(table, xh)
        spectra_ref[b] = (both[:rows] + (both[rows:] + mm(high, xl))).astype(BF16)
    size = 256
    per = size // blocks
    to = lax.broadcasted_iota(jnp.int32, (size, size), 0)
    at = lax.broadcasted_iota(jnp.int32, (size, size), 1)
    order = jnp.where((at % per) * blocks + at // per == to, 1.0, 0.0).astype(BF16)
    for g in range(rows // per):
        group = spectra_ref[:, g * per : (g + 1) * per].reshape(size, -1)
        out_ref[g * size : (g + 1) * size] = mm(order, group).astype(BF16)


def dft(snapshots, freqs):
    blocks, steps, pts = snapshots.shape
    table = make_table(freqs, steps)
    wide = 256
    rows = 2 * freqs
    return pl.pallas_call(
        dft_kernel,
        grid=(pts // wide,),
        in_specs=[
            pl.BlockSpec((2 * rows, steps), lambda i: (0, 0)),
            pl.BlockSpec((blocks, steps, wide), lambda i: (0, 0, i)),
        ],
        out_specs=pl.BlockSpec((rows * blocks, wide), lambda i: (0, i)),
        out_shape=jax.ShapeDtypeStruct((rows * blocks, pts), BF16),
        scratch_shapes=[pltpu.VMEM((blocks, rows, wide), BF16)],
        compiler_params=pltpu.CompilerParams(vmem_limit_bytes=VMEM_LIMIT),
        name="dft",
    )(jnp.asarray(table), snapshots)


def exchange(x, sign_first):
    lane = lax.broadcasted_iota(jnp.int32, x.shape, x.ndim - 1)
    last = x.ndim - 1
    up = pltpu.roll(x, 120, last)
    down = pltpu.roll(x, 8, last)
    if sign_first:
        return jnp.where((lane & 8) == 0, -up, down)
    return jnp.where((lane & 8) == 0, up, -down)


def places(rows):
    row = lax.broadcasted_iota(jnp.int32, (rows, 128), 0)
    lane = lax.broadcasted_iota(jnp.int32, (rows, 128), 1)
    return row, (lane >> 4) * 8 + (lane & 7), (lane & 8) == 0


def gram_kernel(points_all, z_ref, w_ref, out_ref):
    groups, freqs, pairs, pts = z_ref.shape
    weights = w_ref[...]
    rows = groups * pairs // 2
    row, block, first = places(rows)
    for f in range(freqs):
        z = z_ref[:, f].reshape(groups * pairs, pts)
        zw = (z.astype(F32) * weights).astype(BF16)
        m = mm(zw, z, NT).reshape(groups, 2, pairs // 2, 128)
        top = m[:, 0].reshape(rows, 128)
        bottom = m[:, 1].reshape(rows, 128)
        g = (top + exchange(bottom, False)) * (1.0 / points_all)
        p = jnp.where(row <= block, g, pltpu.roll(g, 120, 1))
        half = rows // 2
        out_ref[f] = jnp.where(first[:half], p[:half], pltpu.roll(p[half:], 8, 1)).astype(out_ref.dtype)


def call(kernel, out_shape, *args, scratch=(), name):
    vmem = pl.BlockSpec(memory_space=pltpu.VMEM)
    smem = pl.BlockSpec(memory_space=pltpu.SMEM)
    return pl.pallas_call(
        kernel,
        in_specs=[smem if x.dtype == jnp.int32 else vmem for x in args],
        out_specs=jax.tree.map(lambda _: vmem, out_shape),
        out_shape=out_shape,
        scratch_shapes=scratch,
        compiler_params=pltpu.CompilerParams(vmem_limit_bytes=VMEM_LIMIT),
        name=name,
    )(*args)


def total_kernel(x_ref, out_ref):
    total = jnp.sum(x_ref[...].astype(F32), 0).astype(out_ref.dtype)
    for i in range(out_ref.shape[0]):
        out_ref[i] = total


def factor_out(image):
    cross = mm(image, image, NT, lax.Precision.HIGHEST)
    columns = [jnp.broadcast_to(cross[:, k : k + 1], image.shape) for k in range(KM)]
    row = lax.broadcasted_iota(jnp.int32, image.shape, 0)
    pivots = columns[KM - 1]
    for k in range(KM):
        pivot = columns[k][k : k + 1]
        pivots = jnp.where(row == k, pivot, pivots)
        if k < KM - 1:
            factor = jnp.where(row > k, columns[k] * (1.0 / pivot), 0.0)
            for j in range(k + 1, KM):
                columns[j] = columns[j] - factor * columns[j][k : k + 1]
            image = image - factor * image[k : k + 1]
    return image * lax.rsqrt(pivots)


def unpacked(s):
    half = s.shape[0]
    rows = 2 * half
    row, block, first = places(rows)
    p = jnp.concatenate([s, pltpu.roll(s, 120, 1)], 0)
    tall = (rows // 8, 8, 128)
    t = jnp.stack([p.reshape(tall), p.reshape(tall)], 1).reshape(2 * rows, 128).T
    pt = t.reshape(rows // 8, 2, 8, 128)[:, 0].reshape(rows, 128)
    real = jnp.where(row <= block, p, pt)
    imag = jnp.where(row > block, -p, jnp.where(row == block, 0.0, pt))
    top = jnp.where(first, real, pltpu.roll(-imag, 8, 1))
    bottom = jnp.where(first, imag, pltpu.roll(real, 8, 1))
    return jnp.stack([top.reshape(tall), bottom.reshape(tall)], 1).reshape(2 * rows, 128), top


def iterate(s):
    embedded, top = unpacked(s)
    eh, el = split(embedded)
    e = jnp.concatenate([eh, el], 1)

    def times_e(basis):
        high, low = split(basis)
        r = mm(jnp.concatenate([high, low], 0), e)
        return r[:KM, :128], r[KM:, :128] + r[:KM, 128:]

    image = sum(times_e(top[:KM]))
    basis = factor_out(image)
    basis = factor_out(sum(times_e(sum(times_e(basis)))))
    high, low = split(basis)
    r = mm(jnp.concatenate([high, low], 0), e)
    e_coef = r[:KM, :128] + r[:KM, 128:]
    e_basis = e_coef + r[KM:, :128]
    energy = jnp.sum(high.astype(F32) * e_coef, 1, keepdims=True)
    quotient = jnp.sum(basis * e_basis, 1, keepdims=True)
    lane = lax.broadcasted_iota(jnp.int32, (KM, 128), 1)
    rest = jnp.where(lane < 3, lax.rsqrt(jnp.maximum(energy, 0.0) + 1e-06), quotient)
    first = rest.astype(BF16).astype(F32)
    second = (rest - first).astype(BF16).astype(F32)
    third = rest - first - second
    step = jnp.where(lane < 3, lane, lane - 3)
    words = jnp.where(step == 0, first, jnp.where(step == 1, second, third))
    return jnp.concatenate([high, jnp.where(lane < 6, words, 0.0).astype(BF16)], 0)


def iterate_kernel(x_ref, out_ref):
    total = jnp.sum(x_ref[...].astype(F32), 0)
    for f in range(x_ref.shape[1]):
        result = iterate(total[f])
        for i in range(out_ref.shape[0]):
            out_ref[i, f] = result


def modes_kernel(counts_ref, coef_ref, z_ref, modes_ref, values_ref):
    groups, freqs, pairs, pts = z_ref.shape
    row = lax.broadcasted_iota(jnp.int32, (KM, 128), 0)
    lane = lax.broadcasted_iota(jnp.int32, (KM, 128), 1)
    quotients = jnp.zeros((KM, 128), F32)
    for f in range(freqs):
        coef = coef_ref[f, :KM].astype(F32)
        words = coef_ref[f, KM:].astype(F32)
        keep = row[:, :1] < counts_ref[f]
        scale = jnp.where(keep, words[:, 0:1] + words[:, 1:2] + words[:, 2:3], 0.0)
        quotient = jnp.where(keep, words[:, 3:4] + words[:, 4:5] + words[:, 5:6], 0.0)
        quotients = jnp.where(lane == f, quotient, quotients)
        both = jnp.concatenate([coef, exchange(coef, False)], 0).astype(BF16)
        field = mm(both, z_ref[:, f].reshape(groups * pairs, pts))
        modes_ref[f] = (field * jnp.concatenate([scale, scale], 0)).astype(BF16)
    padded = jnp.concatenate([quotients] * (128 // KM), 0)
    values_ref[...] = padded.T[:freqs, :KM]


def local(snapshots, weights, counts):
    blk_dev, steps, pts = snapshots.shape
    groups = lax.axis_size("blk")
    band = counts.shape[0]
    freqs = band * groups
    far, near = "far", ("near", "x")
    nfar, nnear = lax.axis_size(far), lax.axis_size(near)
    shape = jax.ShapeDtypeStruct
    spectra = dft(snapshots, freqs).reshape(groups, band, 2 * blk_dev, pts)
    own = lax.all_to_all(spectra, "blk", split_axis=0, concat_axis=0, tiled=True)
    half = groups * blk_dev // 2
    each = band // nnear
    packed = call(
        functools.partial(gram_kernel, pts * nfar * nnear),
        shape((band, half, 128), BF16),
        own,
        weights.reshape(1, pts),
        name="gram",
    )
    parts = packed.reshape(nnear, each, half, 128)
    parts = lax.all_to_all(parts, near, split_axis=0, concat_axis=0, tiled=True)
    copies = call(total_kernel, shape((nfar, each, half, 128), BF16), parts, name="total")
    columns = lax.all_to_all(copies, far, split_axis=0, concat_axis=0, tiled=True)
    mine = call(iterate_kernel, shape((nnear, each, 2 * KM, 128), BF16), columns, name="iterate")
    coefs = lax.all_to_all(mine, near, split_axis=0, concat_axis=0, tiled=True)
    coefs = coefs.reshape(band, 2 * KM, 128)
    modes, values = call(
        modes_kernel,
        [shape((band, 2 * KM, pts), BF16), shape((band, KM), F32)],
        counts,
        coefs,
        own,
        name="modes",
    )
    return modes.reshape(band, 2, KM, pts), values


def solution(mesh):
    blk, sp = mesh.devices.shape
    nx, near = 4, 2
    devices = mesh.devices.reshape(blk, sp // (near * nx), near, nx)
    mesh = jax.sharding.Mesh(devices, ("blk", "far", "near", "x"))
    points = ("far", "near", "x")
    in_specs = (P("blk", None, points), P(points), P("blk"))
    out_specs = (P("blk", None, None, points), P("blk", None))
    return jax.shard_map(local, mesh=mesh, in_specs=in_specs, out_specs=out_specs, check_vma=False)
```

```python
import functools

import jax
import jax.numpy as jnp
import ml_dtypes
import numpy as np
from jax import lax
from jax.experimental import pallas as pl
from jax.experimental.pallas import tpu as pltpu
from jax.sharding import PartitionSpec as P

KM = 16
F32 = jnp.float32
BF16 = jnp.bfloat16
NN = (((1,), (0,)), ((), ()))
NT = (((1,), (1,)), ((), ()))
GROUPS = 8
PARTS = 2
VMEM_LIMIT = 48 * 1024 * 1024


def make_table(freqs, steps):
    times = np.arange(steps)
    phase = (np.arange(freqs)[:, None] * times[None, :]) % steps
    angle = 2.0 * np.pi * phase / steps
    window = np.sqrt(8.0 / (3.0 * steps)) * 0.5 * (1.0 - np.cos(2.0 * np.pi * times / steps))
    table = np.stack([np.cos(angle) * window, np.sin(angle) * window], 1)
    table = table.reshape(2 * freqs, steps).astype(np.float32)
    high = table.astype(ml_dtypes.bfloat16)
    low = (table - high.astype(np.float32)).astype(ml_dtypes.bfloat16)
    return np.concatenate([high, low], 0)


def split(x):
    high = x.astype(BF16)
    return high, (x - high.astype(F32)).astype(BF16)


def mm(a, b, dims=NN, precision=None):
    return lax.dot_general(a, b, dims, preferred_element_type=F32, precision=precision)


def dft_kernel(ids_ref, table_ref, x_ref, *refs):
    out_refs, acc_ref = refs[:-1], refs[-1]
    blocks = x_ref.shape[0]
    rows = table_ref.shape[0] // 2
    high, low = table_ref[:rows], table_ref[rows:]
    table = jnp.concatenate([high, low, high], 1)
    for b in range(blocks):
        xh, xl = split(x_ref[b])
        acc = mm(table, jnp.concatenate([xh, xh, xl], 0))
        for col in range(0, acc.shape[1], 128):
            acc_ref[col // 128, pl.ds(b, rows, stride=blocks), :] = acc[:, col : col + 128]
    for mask, out_ref in enumerate(out_refs):
        size = out_ref.shape[0]
        start = pl.multiple_of((ids_ref[0] ^ mask) * size, size)
        for col in range(0, out_ref.shape[1], 128):
            out_ref[:, col : col + 128] = acc_ref[col // 128, pl.ds(start, size), :].astype(BF16)


def dft(ids, snapshots, groups, freqs, part, parts):
    blocks, steps, pts = snapshots.shape
    table = make_table(freqs, steps)
    wide = pts // parts
    rows = 2 * freqs
    size = rows * blocks // groups
    return pl.pallas_call(
        dft_kernel,
        grid=(1,),
        in_specs=[
            pl.BlockSpec(memory_space=pltpu.SMEM),
            pl.BlockSpec((2 * rows, steps), lambda i: (0, 0)),
            pl.BlockSpec((blocks, steps, wide), lambda i: (0, 0, part)),
        ],
        out_specs=[pl.BlockSpec((size, wide), lambda i: (0, 0))] * groups,
        out_shape=[jax.ShapeDtypeStruct((size, wide), BF16)] * groups,
        scratch_shapes=[pltpu.VMEM((wide // 128, rows * blocks, 128), F32)],
        compiler_params=pltpu.CompilerParams(vmem_limit_bytes=VMEM_LIMIT),
        cost_estimate=pl.CostEstimate(
            flops=6 * rows * steps * blocks * wide, bytes_accessed=4 * 1024 * 1024, transcendentals=0
        ),
        name="dft",
    )(ids, jnp.asarray(table), snapshots)


def exchange(x, sign_first):
    lane = lax.broadcasted_iota(jnp.int32, x.shape, x.ndim - 1)
    last = x.ndim - 1
    up = pltpu.roll(x, 120, last)
    down = pltpu.roll(x, 8, last)
    if sign_first:
        return jnp.where((lane & 8) == 0, -up, down)
    return jnp.where((lane & 8) == 0, up, -down)


def places(rows):
    row = lax.broadcasted_iota(jnp.int32, (rows, 128), 0)
    lane = lax.broadcasted_iota(jnp.int32, (rows, 128), 1)
    return row, (lane >> 4) * 8 + (lane & 7), (lane & 8) == 0


def rows_of(z_refs, parts, f, freqs):
    groups = len(z_refs) // parts
    pairs = z_refs[0].shape[0] // freqs
    start = f * pairs if isinstance(f, int) else pl.multiple_of(f * pairs, pairs)
    pieces = []
    for part in range(parts):
        refs = z_refs[part * groups : (part + 1) * groups]
        pieces.append(jnp.concatenate([ref[pl.ds(start, pairs)] for ref in refs], 0))
    return jnp.concatenate(pieces, 1)


def gram_kernel(points_all, parts, ids_ref, w_ref, *refs):
    nnear = len(refs) - 1 - parts * GROUPS
    z_refs, out_refs, all_ref = refs[: parts * GROUPS], refs[-1 - nnear : -1], refs[-1]
    freqs = all_ref.shape[0]
    weights = w_ref[...]
    rows = 8 * GROUPS
    row, block, first = places(rows)
    for f in range(freqs):
        z = rows_of(z_refs, parts, f, freqs)
        zw = (z.astype(F32) * weights).astype(BF16)
        m = mm(zw, z, NT).reshape(GROUPS, 2, 8, 128)
        top = m[:, 0].reshape(rows, 128)
        bottom = m[:, 1].reshape(rows, 128)
        g = (top + exchange(bottom, False)) * (1.0 / points_all)
        p = jnp.where(row <= block, g, pltpu.roll(g, 120, 1))
        half = rows // 2
        all_ref[f] = jnp.where(first[:half], p[:half], pltpu.roll(p[half:], 8, 1)).astype(BF16)
    each = freqs // nnear
    for mask, out_ref in enumerate(out_refs):
        out_ref[...] = all_ref[pl.ds((ids_ref[1] ^ mask) * each, each)]


def call(kernel, out_shape, *args, scratch=(), name):
    vmem = pl.BlockSpec(memory_space=pltpu.VMEM)
    smem = pl.BlockSpec(memory_space=pltpu.SMEM)
    return pl.pallas_call(
        kernel,
        in_specs=[smem if x.dtype == jnp.int32 else vmem for x in args],
        out_specs=jax.tree.map(lambda _: vmem, out_shape),
        out_shape=out_shape,
        scratch_shapes=scratch,
        compiler_params=pltpu.CompilerParams(vmem_limit_bytes=VMEM_LIMIT),
        name=name,
    )(*args)


def total_kernel(*refs):
    total = refs[0][...].astype(F32)
    for ref in refs[1:-1]:
        total = total + ref[...].astype(F32)
    refs[-1][...] = total.astype(BF16)


def factor_out(images):
    images = list(images)
    every = range(len(images))
    cross = [mm(x, x, NT, lax.Precision.HIGHEST) for x in images]
    columns = [[jnp.broadcast_to(c[:, k : k + 1], (KM, 128)) for k in range(KM)] for c in cross]
    row = lax.broadcasted_iota(jnp.int32, (KM, 128), 0)
    pivots = [columns[f][KM - 1] for f in every]
    for k in range(KM):
        for f in every:
            pivot = columns[f][k][k : k + 1]
            pivots[f] = jnp.where(row == k, pivot, pivots[f])
            if k < KM - 1:
                factor = jnp.where(row > k, columns[f][k] * (1.0 / pivot), 0.0)
                for j in range(k + 1, KM):
                    columns[f][j] = columns[f][j] - factor * columns[f][j][k : k + 1]
                images[f] = images[f] - factor * images[f][k : k + 1]
    return [x * lax.rsqrt(p) for x, p in zip(images, pivots)]


def unpacked(s):
    half = s.shape[0]
    rows = 2 * half
    row, block, first = places(rows)
    p = jnp.concatenate([s, pltpu.roll(s, 120, 1)], 0)
    tall = (rows // 8, 8, 128)
    t = jnp.stack([p.reshape(tall), p.reshape(tall)], 1).reshape(2 * rows, 128).T
    pt = t.reshape(rows // 8, 2, 8, 128)[:, 0].reshape(rows, 128)
    real = jnp.where(row <= block, p, pt)
    imag = jnp.where(row > block, -p, jnp.where(row == block, 0.0, pt))
    top = jnp.where(first, real, pltpu.roll(-imag, 8, 1))
    bottom = jnp.where(first, imag, pltpu.roll(real, 8, 1))
    return jnp.stack([top.reshape(tall), bottom.reshape(tall)], 1).reshape(2 * rows, 128), top


def iterate_kernel(ids_ref, *refs):
    x_refs, out_ref, x_ref, top_ref = refs[:-3], refs[-3], refs[-2], refs[-1]
    for mask, ref in enumerate(x_refs):
        x_ref[ids_ref[2] ^ mask] = ref[...].astype(F32)
    total = jnp.sum(x_ref[...], 0)
    every = range(total.shape[0])
    e, starts = [], []
    for f in every:
        embedded, top = unpacked(total[f])
        e.append(jnp.concatenate(split(embedded), 1))
        top_ref[f] = top
    for f in every:
        at = [pl.multiple_of((ids_ref[0] ^ s) * 8, 8) for s in range(KM // 8)]
        starts.append(jnp.concatenate([top_ref[f, pl.ds(i, 8), :] for i in at], 0))

    def products(basis):
        r = [mm(jnp.concatenate(split(x), 0), e[f]) for f, x in enumerate(basis)]
        return [(x[:KM, :128], x[KM:, :128], x[:KM, 128:]) for x in r]

    def times_e(basis):
        return [a + (b + c) for a, b, c in products(basis)]

    basis = factor_out(times_e(starts))
    basis = factor_out(times_e(times_e(basis)))
    lane = lax.broadcasted_iota(jnp.int32, (KM, 128), 1)
    for f, (a, b, c) in enumerate(products(basis)):
        high = basis[f].astype(BF16)
        energy = jnp.sum(high.astype(F32) * (a + c), 1, keepdims=True)
        quotient = jnp.sum(basis[f] * (a + (b + c)), 1, keepdims=True)
        rest = jnp.where(lane < 3, lax.rsqrt(jnp.maximum(energy, 0.0) + 1e-06), quotient)
        first = rest.astype(BF16).astype(F32)
        second = (rest - first).astype(BF16).astype(F32)
        third = rest - first - second
        step = jnp.where(lane < 3, lane, lane - 3)
        words = jnp.where(step == 0, first, jnp.where(step == 1, second, third))
        out_ref[f] = jnp.concatenate([high, jnp.where(lane < 6, words, 0.0).astype(BF16)], 0)


def modes_kernel(parts, ids_ref, counts_ref, *refs):
    modes_ref, values_ref = refs[-2:]
    z_refs, coef_refs = refs[: parts * GROUPS], refs[parts * GROUPS : -2]
    freqs = counts_ref.shape[0]
    each = coef_refs[0].shape[0]
    row = lax.broadcasted_iota(jnp.int32, (KM, 128), 0)
    lane = lax.broadcasted_iota(jnp.int32, (KM, 128), 1)
    quotients = jnp.zeros((KM, 128), F32)
    for mask, ref in enumerate(coef_refs):
        for i in range(each):
            f = (ids_ref[1] ^ mask) * each + i
            coef = ref[i, :KM].astype(F32)
            words = ref[i, KM:].astype(F32)
            keep = row[:, :1] < counts_ref[f]
            scale = jnp.where(keep, words[:, 0:1] + words[:, 1:2] + words[:, 2:3], 0.0)
            quotient = jnp.where(keep, words[:, 3:4] + words[:, 4:5] + words[:, 5:6], 0.0)
            quotients = jnp.where(lane == f, quotient, quotients)
            both = jnp.concatenate([coef, exchange(coef, False)], 0).astype(BF16)
            field = mm(both, rows_of(z_refs, parts, f, freqs))
            modes_ref[f] = (field * jnp.concatenate([scale, scale], 0)).astype(BF16)
    padded = jnp.concatenate([quotients] * (128 // KM), 0)
    values_ref[...] = padded.T[:freqs, :KM]


def swap(pieces, axis):
    size = lax.axis_size(axis)
    moved = [lax.ppermute(pieces[m], axis, [(i, i ^ m) for i in range(size)]) for m in range(1, size)]
    return [pieces[0]] + moved


def local(snapshots, weights, counts):
    pts = snapshots.shape[2]
    groups = lax.axis_size("blk")
    band = counts.shape[0]
    far, near = "far", ("near", "x")
    nfar, nnear = lax.axis_size(far), lax.axis_size(near)
    ids = jnp.stack([lax.axis_index("blk"), lax.axis_index(near), lax.axis_index(far)]).astype(jnp.int32)
    shape = jax.ShapeDtypeStruct
    each, half = band // nnear, 4 * GROUPS
    own = []
    for part in range(PARTS):
        own += swap(dft(ids, snapshots, groups, band * groups, part, PARTS), "blk")
    packed = call(
        functools.partial(gram_kernel, pts * nfar * nnear, PARTS),
        [shape((each, half, 128), BF16)] * nnear,
        ids,
        weights.reshape(1, pts),
        *own,
        scratch=[pltpu.VMEM((band, half, 128), BF16)],
        name="gram",
    )
    mine = call(total_kernel, shape((each, half, 128), BF16), *swap(packed, near), name="total")
    coefs = call(
        iterate_kernel,
        shape((each, 2 * KM, 128), BF16),
        ids,
        *swap([mine] * nfar, far),
        scratch=[pltpu.VMEM((nfar, each, half, 128), F32), pltpu.VMEM((each, 2 * half, 128), F32)],
        name="iterate",
    )
    modes, values = call(
        functools.partial(modes_kernel, PARTS),
        [shape((band, 2 * KM, pts), BF16), shape((band, KM), F32)],
        ids,
        counts,
        *own,
        *swap([coefs] * nnear, near),
        name="modes",
    )
    return modes.reshape(band, 2, KM, pts), values


def solution(mesh):
    blk, sp = mesh.devices.shape
    nx, near = 4, 2
    devices = mesh.devices.reshape(blk, sp // (near * nx), near, nx)
    mesh = jax.sharding.Mesh(devices, ("blk", "far", "near", "x"))
    points = ("far", "near", "x")
    in_specs = (P("blk", None, points), P(points), P("blk"))
    out_specs = (P("blk", None, None, points), P("blk", None))
    return jax.shard_map(local, mesh=mesh, in_specs=in_specs, out_specs=out_specs, check_vma=False)
```

```python
import functools
import math

import jax
import jax.numpy as jnp
from jax import lax
from jax.experimental import pallas as pl
from jax.experimental.pallas import tpu as pltpu
from jax.sharding import PartitionSpec as P

KM = 16
F32 = jnp.float32
BF16 = jnp.bfloat16
NN = (((1,), (0,)), ((), ()))
NT = (((1,), (1,)), ((), ()))
VMEM_LIMIT = 48 * 1024 * 1024


def sine(x):
    square = x * x
    total = jnp.full_like(x, 1.0 / math.factorial(13))
    for n in (11, 9, 7, 5, 3, 1):
        total = total * square + (1.0 if n % 4 == 1 else -1.0) / math.factorial(n)
    return total * x


def make_table(rows, steps):
    row = lax.broadcasted_iota(jnp.int32, (rows, steps), 0)
    time = lax.broadcasted_iota(jnp.int32, (rows, steps), 1)
    phase = (row >> 1) * time - (row & 1) * (steps // 4)
    phase = ((phase + steps // 2) & (steps - 1)) - steps // 2
    half = sine(phase.astype(F32) * (math.pi / steps))
    time = lax.broadcasted_iota(jnp.int32, (8, steps), 1)
    window = sine((time - steps // 2).astype(F32) * (math.pi / steps))
    window = math.sqrt(8.0 / (3.0 * steps)) * (1.0 - window * window)
    return (1.0 - 2.0 * half * half) * window[:1]


def split(x):
    high = x.astype(BF16)
    return high, (x - high.astype(F32)).astype(BF16)


def mm(a, b, dims=NN, precision=None):
    return lax.dot_general(a, b, dims, preferred_element_type=F32, precision=precision)


def dft_kernel(x_ref, out_ref, table_ref, acc_ref):
    blocks, steps = x_ref.shape[:2]
    rows = table_ref.shape[0]

    @pl.when(pl.program_id(0) == 0)
    def _():
        high, low = split(make_table(rows, steps))
        table_ref[:, :steps] = high
        table_ref[:, steps : 2 * steps] = low
        table_ref[:, 2 * steps :] = high

    for b in range(blocks):
        xh, xl = split(x_ref[b])
        acc = mm(table_ref[...], jnp.concatenate([xh, xh, xl], 0))
        for col in range(0, acc.shape[1], 128):
            acc_ref[col // 128, pl.ds(b, rows, stride=blocks), :] = acc[:, col : col + 128]
    for col in range(0, out_ref.shape[1], 128):
        out_ref[:, col : col + 128] = acc_ref[col // 128].astype(BF16)


def dft(snapshots, freqs):
    blocks, steps, pts = snapshots.shape
    wide = 256
    rows = 2 * freqs
    return pl.pallas_call(
        dft_kernel,
        grid=(pts // wide,),
        in_specs=[pl.BlockSpec((blocks, steps, wide), lambda i: (0, 0, i))],
        out_specs=pl.BlockSpec((rows * blocks, wide), lambda i: (0, i)),
        out_shape=jax.ShapeDtypeStruct((rows * blocks, pts), BF16),
        scratch_shapes=[
            pltpu.VMEM((rows, 3 * steps), BF16),
            pltpu.VMEM((wide // 128, rows * blocks, 128), F32),
        ],
        compiler_params=pltpu.CompilerParams(vmem_limit_bytes=VMEM_LIMIT),
        name="dft",
    )(snapshots)


def exchange(x, sign_first):
    lane = lax.broadcasted_iota(jnp.int32, x.shape, x.ndim - 1)
    last = x.ndim - 1
    up = pltpu.roll(x, 120, last)
    down = pltpu.roll(x, 8, last)
    if sign_first:
        return jnp.where((lane & 8) == 0, -up, down)
    return jnp.where((lane & 8) == 0, up, -down)


def places(rows):
    row = lax.broadcasted_iota(jnp.int32, (rows, 128), 0)
    lane = lax.broadcasted_iota(jnp.int32, (rows, 128), 1)
    return row, (lane >> 4) * 8 + (lane & 7), (lane & 8) == 0


def gram_kernel(points_all, z_ref, w_ref, out_ref):
    groups, freqs, pairs, pts = z_ref.shape
    weights = w_ref[...]
    rows = groups * pairs // 2
    row, block, first = places(rows)
    for f in range(freqs):
        z = z_ref[:, f].reshape(groups * pairs, pts)
        zw = (z.astype(F32) * weights).astype(BF16)
        m = mm(zw, z, NT).reshape(groups, 2, pairs // 2, 128)
        top = m[:, 0].reshape(rows, 128)
        bottom = m[:, 1].reshape(rows, 128)
        g = (top + exchange(bottom, False)) * (1.0 / points_all)
        p = jnp.where(row <= block, g, pltpu.roll(g, 120, 1))
        half = rows // 2
        out_ref[f] = jnp.where(first[:half], p[:half], pltpu.roll(p[half:], 8, 1)).astype(out_ref.dtype)


def call(kernel, out_shape, *args, scratch=(), name):
    vmem = pl.BlockSpec(memory_space=pltpu.VMEM)
    smem = pl.BlockSpec(memory_space=pltpu.SMEM)
    return pl.pallas_call(
        kernel,
        in_specs=[smem if x.dtype == jnp.int32 else vmem for x in args],
        out_specs=jax.tree.map(lambda _: vmem, out_shape),
        out_shape=out_shape,
        scratch_shapes=scratch,
        compiler_params=pltpu.CompilerParams(vmem_limit_bytes=VMEM_LIMIT),
        name=name,
    )(*args)


def total_kernel(x_ref, out_ref):
    total = jnp.sum(x_ref[...].astype(F32), 0).astype(out_ref.dtype)
    for i in range(out_ref.shape[0]):
        out_ref[i] = total


def factor_out(images):
    images = list(images)
    every = range(len(images))
    cross = [mm(x, x, NT, lax.Precision.HIGHEST) for x in images]
    columns = [[jnp.broadcast_to(c[:, k : k + 1], (KM, 128)) for k in range(KM)] for c in cross]
    row = lax.broadcasted_iota(jnp.int32, (KM, 128), 0)
    pivots = [columns[f][KM - 1] for f in every]
    for k in range(KM):
        for f in every:
            pivot = columns[f][k][k : k + 1]
            pivots[f] = jnp.where(row == k, pivot, pivots[f])
            if k < KM - 1:
                factor = jnp.where(row > k, columns[f][k] * (1.0 / pivot), 0.0)
                for j in range(k + 1, KM):
                    columns[f][j] = columns[f][j] - factor * columns[f][j][k : k + 1]
                images[f] = images[f] - factor * images[f][k : k + 1]
    return [x * lax.rsqrt(p) for x, p in zip(images, pivots)]


def unpacked(s):
    half = s.shape[0]
    rows = 2 * half
    row, block, first = places(rows)
    p = jnp.concatenate([s, pltpu.roll(s, 120, 1)], 0)
    tall = (rows // 8, 8, 128)
    t = jnp.stack([p.reshape(tall), p.reshape(tall)], 1).reshape(2 * rows, 128).T
    pt = t.reshape(rows // 8, 2, 8, 128)[:, 0].reshape(rows, 128)
    real = jnp.where(row <= block, p, pt)
    imag = jnp.where(row > block, -p, jnp.where(row == block, 0.0, pt))
    top = jnp.where(first, real, pltpu.roll(-imag, 8, 1))
    bottom = jnp.where(first, imag, pltpu.roll(real, 8, 1))
    return jnp.stack([top.reshape(tall), bottom.reshape(tall)], 1).reshape(2 * rows, 128), top


def iterate_kernel(x_ref, out_ref):
    total = jnp.sum(x_ref[...].astype(F32), 0)
    every = range(total.shape[0])
    e, starts = [], []
    for f in every:
        embedded, top = unpacked(total[f])
        e.append(jnp.concatenate(split(embedded), 1))
        starts.append(top[:KM])

    def products(basis):
        r = [mm(jnp.concatenate(split(x), 0), e[f]) for f, x in enumerate(basis)]
        return [(x[:KM, :128], x[KM:, :128], x[:KM, 128:]) for x in r]

    def times_e(basis):
        return [a + (b + c) for a, b, c in products(basis)]

    basis = factor_out(times_e(starts))
    basis = factor_out(times_e(times_e(basis)))
    lane = lax.broadcasted_iota(jnp.int32, (KM, 128), 1)
    for f, (a, b, c) in enumerate(products(basis)):
        high = basis[f].astype(BF16)
        energy = jnp.sum(high.astype(F32) * (a + c), 1, keepdims=True)
        quotient = jnp.sum(basis[f] * (a + (b + c)), 1, keepdims=True)
        rest = jnp.where(lane < 3, lax.rsqrt(jnp.maximum(energy, 0.0) + 1e-06), quotient)
        first = rest.astype(BF16).astype(F32)
        second = (rest - first).astype(BF16).astype(F32)
        third = rest - first - second
        step = jnp.where(lane < 3, lane, lane - 3)
        words = jnp.where(step == 0, first, jnp.where(step == 1, second, third))
        result = jnp.concatenate([high, jnp.where(lane < 6, words, 0.0).astype(BF16)], 0)
        for i in range(out_ref.shape[0]):
            out_ref[i, f] = result


def modes_kernel(counts_ref, coef_ref, z_ref, modes_ref, values_ref):
    groups, freqs, pairs, pts = z_ref.shape
    row = lax.broadcasted_iota(jnp.int32, (KM, 128), 0)
    lane = lax.broadcasted_iota(jnp.int32, (KM, 128), 1)
    quotients = jnp.zeros((KM, 128), F32)
    for f in range(freqs):
        coef = coef_ref[f, :KM].astype(F32)
        words = coef_ref[f, KM:].astype(F32)
        keep = row[:, :1] < counts_ref[f]
        scale = jnp.where(keep, words[:, 0:1] + words[:, 1:2] + words[:, 2:3], 0.0)
        quotient = jnp.where(keep, words[:, 3:4] + words[:, 4:5] + words[:, 5:6], 0.0)
        quotients = jnp.where(lane == f, quotient, quotients)
        both = jnp.concatenate([coef, exchange(coef, False)], 0).astype(BF16)
        field = mm(both, z_ref[:, f].reshape(groups * pairs, pts))
        modes_ref[f] = (field * jnp.concatenate([scale, scale], 0)).astype(BF16)
    padded = jnp.concatenate([quotients] * (128 // KM), 0)
    values_ref[...] = padded.T[:freqs, :KM]


def local(snapshots, weights, counts):
    blk_dev, steps, pts = snapshots.shape
    groups = lax.axis_size("blk")
    band = counts.shape[0]
    freqs = band * groups
    far, near = "far", ("near", "x")
    nfar, nnear = lax.axis_size(far), lax.axis_size(near)
    shape = jax.ShapeDtypeStruct
    spectra = dft(snapshots, freqs).reshape(groups, band, 2 * blk_dev, pts)
    own = lax.all_to_all(spectra, "blk", split_axis=0, concat_axis=0, tiled=True)
    half = groups * blk_dev // 2
    each = band // nnear
    packed = call(
        functools.partial(gram_kernel, pts * nfar * nnear),
        shape((band, half, 128), BF16),
        own,
        weights.reshape(1, pts),
        name="gram",
    )
    parts = packed.reshape(nnear, each, half, 128)
    parts = lax.all_to_all(parts, near, split_axis=0, concat_axis=0, tiled=True)
    copies = call(total_kernel, shape((nfar, each, half, 128), BF16), parts, name="total")
    columns = lax.all_to_all(copies, far, split_axis=0, concat_axis=0, tiled=True)
    mine = call(iterate_kernel, shape((nnear, each, 2 * KM, 128), BF16), columns, name="iterate")
    coefs = lax.all_to_all(mine, near, split_axis=0, concat_axis=0, tiled=True)
    coefs = coefs.reshape(band, 2 * KM, 128)
    modes, values = call(
        modes_kernel,
        [shape((band, 2 * KM, pts), BF16), shape((band, KM), F32)],
        counts,
        coefs,
        own,
        name="modes",
    )
    return modes.reshape(band, 2, KM, pts), values


def solution(mesh):
    blk, sp = mesh.devices.shape
    nx, near = 4, 2
    devices = mesh.devices.reshape(blk, sp // (near * nx), near, nx)
    mesh = jax.sharding.Mesh(devices, ("blk", "far", "near", "x"))
    points = ("far", "near", "x")
    in_specs = (P("blk", None, points), P(points), P("blk"))
    out_specs = (P("blk", None, None, points), P("blk", None))
    return jax.shard_map(local, mesh=mesh, in_specs=in_specs, out_specs=out_specs, check_vma=False)
```

```python
import functools
import math

import jax
import jax.numpy as jnp
from jax import lax
from jax.experimental import pallas as pl
from jax.experimental.pallas import tpu as pltpu
from jax.sharding import PartitionSpec as P

KM = 16
F32 = jnp.float32
BF16 = jnp.bfloat16
NN = (((1,), (0,)), ((), ()))
NT = (((1,), (1,)), ((), ()))
VMEM_LIMIT = 48 * 1024 * 1024


def sine(x):
    square = x * x
    total = jnp.full_like(x, 1.0 / math.factorial(13))
    for n in (11, 9, 7, 5, 3, 1):
        total = total * square + (1.0 if n % 4 == 1 else -1.0) / math.factorial(n)
    return total * x


def make_table(rows, steps):
    row = lax.broadcasted_iota(jnp.int32, (rows, steps), 0)
    time = lax.broadcasted_iota(jnp.int32, (rows, steps), 1)
    phase = (row >> 1) * time - (row & 1) * (steps // 4)
    phase = ((phase + steps // 2) & (steps - 1)) - steps // 2
    half = sine(phase.astype(F32) * (math.pi / steps))
    time = lax.broadcasted_iota(jnp.int32, (8, steps), 1)
    window = sine((time - steps // 2).astype(F32) * (math.pi / steps))
    window = math.sqrt(8.0 / (3.0 * steps)) * (1.0 - window * window)
    return (1.0 - 2.0 * half * half) * window[:1]


def split(x):
    high = x.astype(BF16)
    return high, (x - high.astype(F32)).astype(BF16)


def mm(a, b, dims=NN, precision=None):
    return lax.dot_general(a, b, dims, preferred_element_type=F32, precision=precision)


def dft_kernel(x_hbm, out_ref, table_ref, acc_ref, x_ref, sems):
    blocks, steps, pts = x_hbm.shape
    rows = table_ref.shape[0]
    parts, wide = x_ref.shape[0], x_ref.shape[3]
    fetches = [
        pltpu.make_async_copy(x_hbm.at[:, :, pl.ds(i * wide, wide)], x_ref.at[i], sems.at[i])
        for i in range(parts)
    ]
    for fetch in fetches:
        fetch.start()
    high, low = split(make_table(rows, steps))
    table_ref[:, :steps] = high
    table_ref[:, steps : 2 * steps] = low
    table_ref[:, 2 * steps :] = high
    for i in range(parts):
        fetches[i].wait()
        for b in range(blocks):
            xh, xl = split(x_ref[i, b])
            acc = mm(table_ref[...], jnp.concatenate([xh, xh, xl], 0))
            for col in range(0, wide, 128):
                acc_ref[col // 128, pl.ds(b, rows, stride=blocks), :] = acc[:, col : col + 128]
        for col in range(0, wide, 128):
            at = i * wide + col
            out_ref[:, at : at + 128] = acc_ref[col // 128].astype(BF16)


def dft(snapshots, freqs):
    blocks, steps, pts = snapshots.shape
    wide = 256
    rows = 2 * freqs
    return pl.pallas_call(
        dft_kernel,
        in_specs=[pl.BlockSpec(memory_space=pl.ANY)],
        out_specs=pl.BlockSpec(memory_space=pltpu.VMEM),
        out_shape=jax.ShapeDtypeStruct((rows * blocks, pts), BF16),
        scratch_shapes=[
            pltpu.VMEM((rows, 3 * steps), BF16),
            pltpu.VMEM((wide // 128, rows * blocks, 128), F32),
            pltpu.VMEM((pts // wide, blocks, steps, wide), F32),
            pltpu.SemaphoreType.DMA((pts // wide,)),
        ],
        compiler_params=pltpu.CompilerParams(vmem_limit_bytes=VMEM_LIMIT),
        name="dft",
    )(snapshots)


def exchange(x, sign_first):
    lane = lax.broadcasted_iota(jnp.int32, x.shape, x.ndim - 1)
    last = x.ndim - 1
    up = pltpu.roll(x, 120, last)
    down = pltpu.roll(x, 8, last)
    if sign_first:
        return jnp.where((lane & 8) == 0, -up, down)
    return jnp.where((lane & 8) == 0, up, -down)


def places(rows):
    row = lax.broadcasted_iota(jnp.int32, (rows, 128), 0)
    lane = lax.broadcasted_iota(jnp.int32, (rows, 128), 1)
    return row, (lane >> 4) * 8 + (lane & 7), (lane & 8) == 0


def gram_kernel(points_all, z_ref, w_ref, out_ref):
    groups, freqs, pairs, pts = z_ref.shape
    weights = w_ref[...]
    rows = groups * pairs // 2
    row, block, first = places(rows)
    for f in range(freqs):
        z = z_ref[:, f].reshape(groups * pairs, pts)
        zw = (z.astype(F32) * weights).astype(BF16)
        m = mm(zw, z, NT).reshape(groups, 2, pairs // 2, 128)
        top = m[:, 0].reshape(rows, 128)
        bottom = m[:, 1].reshape(rows, 128)
        g = (top + exchange(bottom, False)) * (1.0 / points_all)
        p = jnp.where(row <= block, g, pltpu.roll(g, 120, 1))
        half = rows // 2
        out_ref[f] = jnp.where(first[:half], p[:half], pltpu.roll(p[half:], 8, 1)).astype(out_ref.dtype)


def call(kernel, out_shape, *args, scratch=(), name):
    vmem = pl.BlockSpec(memory_space=pltpu.VMEM)
    smem = pl.BlockSpec(memory_space=pltpu.SMEM)
    return pl.pallas_call(
        kernel,
        in_specs=[smem if x.dtype == jnp.int32 else vmem for x in args],
        out_specs=jax.tree.map(lambda _: vmem, out_shape),
        out_shape=out_shape,
        scratch_shapes=scratch,
        compiler_params=pltpu.CompilerParams(vmem_limit_bytes=VMEM_LIMIT),
        name=name,
    )(*args)


def total_kernel(x_ref, out_ref):
    total = jnp.sum(x_ref[...].astype(F32), 0).astype(out_ref.dtype)
    for i in range(out_ref.shape[0]):
        out_ref[i] = total


def factor_out(images):
    images = list(images)
    every = range(len(images))
    cross = [mm(x, x, NT, lax.Precision.HIGHEST) for x in images]
    columns = [[jnp.broadcast_to(c[:, k : k + 1], (KM, 128)) for k in range(KM)] for c in cross]
    row = lax.broadcasted_iota(jnp.int32, (KM, 128), 0)
    pivots = [columns[f][KM - 1] for f in every]
    for k in range(KM):
        for f in every:
            pivot = columns[f][k][k : k + 1]
            pivots[f] = jnp.where(row == k, pivot, pivots[f])
            if k < KM - 1:
                factor = jnp.where(row > k, columns[f][k] * (1.0 / pivot), 0.0)
                for j in range(k + 1, KM):
                    columns[f][j] = columns[f][j] - factor * columns[f][j][k : k + 1]
                images[f] = images[f] - factor * images[f][k : k + 1]
    return [x * lax.rsqrt(p) for x, p in zip(images, pivots)]


def unpacked(s):
    half = s.shape[0]
    rows = 2 * half
    row, block, first = places(rows)
    p = jnp.concatenate([s, pltpu.roll(s, 120, 1)], 0)
    tall = (rows // 8, 8, 128)
    t = jnp.stack([p.reshape(tall), p.reshape(tall)], 1).reshape(2 * rows, 128).T
    pt = t.reshape(rows // 8, 2, 8, 128)[:, 0].reshape(rows, 128)
    real = jnp.where(row <= block, p, pt)
    imag = jnp.where(row > block, -p, jnp.where(row == block, 0.0, pt))
    top = jnp.where(first, real, pltpu.roll(-imag, 8, 1))
    bottom = jnp.where(first, imag, pltpu.roll(real, 8, 1))
    return jnp.stack([top.reshape(tall), bottom.reshape(tall)], 1).reshape(2 * rows, 128), top


def iterate_kernel(x_ref, out_ref):
    total = jnp.sum(x_ref[...].astype(F32), 0)
    every = range(total.shape[0])
    e, starts = [], []
    for f in every:
        embedded, top = unpacked(total[f])
        e.append(jnp.concatenate(split(embedded), 1))
        starts.append(top[:KM])

    def products(basis):
        r = [mm(jnp.concatenate(split(x), 0), e[f]) for f, x in enumerate(basis)]
        return [(x[:KM, :128], x[KM:, :128], x[:KM, 128:]) for x in r]

    def times_e(basis):
        return [a + (b + c) for a, b, c in products(basis)]

    basis = factor_out(times_e(starts))
    basis = factor_out(times_e(times_e(basis)))
    lane = lax.broadcasted_iota(jnp.int32, (KM, 128), 1)
    for f, (a, b, c) in enumerate(products(basis)):
        high = basis[f].astype(BF16)
        energy = jnp.sum(high.astype(F32) * (a + c), 1, keepdims=True)
        quotient = jnp.sum(basis[f] * (a + (b + c)), 1, keepdims=True)
        rest = jnp.where(lane < 3, lax.rsqrt(jnp.maximum(energy, 0.0) + 1e-06), quotient)
        first = rest.astype(BF16).astype(F32)
        second = (rest - first).astype(BF16).astype(F32)
        third = rest - first - second
        step = jnp.where(lane < 3, lane, lane - 3)
        words = jnp.where(step == 0, first, jnp.where(step == 1, second, third))
        result = jnp.concatenate([high, jnp.where(lane < 6, words, 0.0).astype(BF16)], 0)
        for i in range(out_ref.shape[0]):
            out_ref[i, f] = result


def modes_kernel(counts_ref, coef_ref, z_ref, modes_ref, values_ref):
    groups, freqs, pairs, pts = z_ref.shape
    row = lax.broadcasted_iota(jnp.int32, (KM, 128), 0)
    lane = lax.broadcasted_iota(jnp.int32, (KM, 128), 1)
    quotients = jnp.zeros((KM, 128), F32)
    for f in range(freqs):
        coef = coef_ref[f, :KM].astype(F32)
        words = coef_ref[f, KM:].astype(F32)
        keep = row[:, :1] < counts_ref[f]
        scale = jnp.where(keep, words[:, 0:1] + words[:, 1:2] + words[:, 2:3], 0.0)
        quotient = jnp.where(keep, words[:, 3:4] + words[:, 4:5] + words[:, 5:6], 0.0)
        quotients = jnp.where(lane == f, quotient, quotients)
        both = jnp.concatenate([coef, exchange(coef, False)], 0).astype(BF16)
        field = mm(both, z_ref[:, f].reshape(groups * pairs, pts))
        modes_ref[f] = (field * jnp.concatenate([scale, scale], 0)).astype(BF16)
    padded = jnp.concatenate([quotients] * (128 // KM), 0)
    values_ref[...] = padded.T[:freqs, :KM]


def local(snapshots, weights, counts):
    blk_dev, steps, pts = snapshots.shape
    groups = lax.axis_size("blk")
    band = counts.shape[0]
    freqs = band * groups
    far, near = "far", ("near", "x")
    nfar, nnear = lax.axis_size(far), lax.axis_size(near)
    shape = jax.ShapeDtypeStruct
    spectra = dft(snapshots, freqs).reshape(groups, band, 2 * blk_dev, pts)
    own = lax.all_to_all(spectra, "blk", split_axis=0, concat_axis=0, tiled=True)
    half = groups * blk_dev // 2
    each = band // nnear
    packed = call(
        functools.partial(gram_kernel, pts * nfar * nnear),
        shape((band, half, 128), BF16),
        own,
        weights.reshape(1, pts),
        name="gram",
    )
    parts = packed.reshape(nnear, each, half, 128)
    parts = lax.all_to_all(parts, near, split_axis=0, concat_axis=0, tiled=True)
    copies = call(total_kernel, shape((nfar, each, half, 128), BF16), parts, name="total")
    columns = lax.all_to_all(copies, far, split_axis=0, concat_axis=0, tiled=True)
    mine = call(iterate_kernel, shape((nnear, each, 2 * KM, 128), BF16), columns, name="iterate")
    coefs = lax.all_to_all(mine, near, split_axis=0, concat_axis=0, tiled=True)
    coefs = coefs.reshape(band, 2 * KM, 128)
    modes, values = call(
        modes_kernel,
        [shape((band, 2 * KM, pts), BF16), shape((band, KM), F32)],
        counts,
        coefs,
        own,
        name="modes",
    )
    return modes.reshape(band, 2, KM, pts), values


def solution(mesh):
    blk, sp = mesh.devices.shape
    nx, near = 4, 2
    devices = mesh.devices.reshape(blk, sp // (near * nx), near, nx)
    mesh = jax.sharding.Mesh(devices, ("blk", "far", "near", "x"))
    points = ("far", "near", "x")
    in_specs = (P("blk", None, points), P(points), P("blk"))
    out_specs = (P("blk", None, None, points), P("blk", None))
    return jax.shard_map(local, mesh=mesh, in_specs=in_specs, out_specs=out_specs, check_vma=False)
```
